1024 devices in a mesh: node: 16 (over y_lo, x, core), expert: 64 (over y_hi, z).
Axes of the slice: x: 4, y: 4 (y_hi: 2, y_lo: 2; y = y_hi * 2 + y_lo), z: 32, core: 2. Of those that a mesh axis runs over, the one named last changes fastest.
Arguments:
- tokens: bfloat16 [4096, 4096], P(('node', 'expert')), may hold values from -6 to 6
- expert_ids: int32 [4096, 8], P(('node', 'expert')), may hold values from 0 to 127, as said below
- gate_units: int32 [4096, 8], P(('node', 'expert')), may hold values from 1 to 16
- slot_ids: int32 [4096, 8], P(('node', 'expert')), may hold values from 0 to 39, as said below
- grad_out: bfloat16 [4096, 4096], P(('node', 'expert')), may hold values from -6 to 6
- gate_weight: bfloat16 [64, 4096, 1536], P('expert', None, 'node'), may hold values from -0.09375 to 0.09375
- up_weight: bfloat16 [64, 4096, 1536], P('expert', None, 'node'), may hold values from -0.09375 to 0.09375
- down_weight: bfloat16 [64, 1536, 4096], P('expert', 'node'), may hold values from -0.21875 to 0.21875
Outputs:
- mixed: bfloat16 [4096, 4096], P(('node', 'expert'))
- grad_tokens: bfloat16 [4096, 4096], P(('node', 'expert'))
- grad_down: bfloat16 [64, 1536, 4096], P('expert', 'node')
The draws below stay inside these ranges and needn't reach their ends.
Inputs may be any that keep to these rules, and one draw needn't show every extreme that they name: `expert_ids`: each token names 8 experts whose indices e // 2 differ; the tokens of one device name each such index at most 1 times; the 256 tokens of one node group name each index exactly 4 * 8 times, and one expert at most 20 times, a bound reached by some expert of each parity in every group. slot_ids[t, k] = (e % 2) * 20 + r with e = expert_ids[t, k] and r below 20; within one node group the choices of one expert have distinct r from 0 upward.
All inputs are finite; a program needn't handle non-finite values.
Results may differ from the reference program's by a relative error of at most 0.012.
Values may be sent and summed in bfloat16 or wider, within the bound.
No kernel may reach another device: no remote copies, remote signals or barrier semaphores. Data moves between devices by JAX's collectives and lax.ppermute only.
A program may use at most 64 MiB of HBM per device.

```python
import jax
import jax.numpy as jnp
from jax import lax

D = 4096
F = 768
TOP = 8
EXP_COL = 2
TOK_DEV = 4
EXPERTS = 128
TOKENS = 4096
SLOTS = 20
N_NODE = 16
N_EXPERT = 64


def routing_tables(key):
    column_count = EXPERTS // EXP_COL
    group_size = TOK_DEV * column_count
    load = TOK_DEV * TOP
    lowest = load - SLOTS
    group_count = TOKENS // group_size

    def one_group(sub):
        keys = jax.random.split(sub, 5)
        lanes = jnp.arange(column_count, dtype=jnp.int32)
        first = jax.random.randint(keys[0], (column_count,), lowest, SLOTS + 1)
        forced = jax.random.randint(keys[1], (), 0, column_count)
        first = jnp.where(lanes == forced, SLOTS, first)
        first = jnp.where(lanes == (forced + 1) % column_count, lowest, first)
        device_perm = jax.random.permutation(keys[2], column_count).astype(jnp.int32)
        column_perm = jax.random.permutation(keys[3], column_count).astype(jnp.int32)
        shifts = jax.random.randint(keys[4], (group_size,), 0, TOP)
        places = jnp.arange(group_size * TOP, dtype=jnp.int32)
        block = places // load
        offset = places % load
        bound = first[block]
        parity = (offset >= bound).astype(jnp.int32)
        rank = offset - parity * bound
        inner = places % group_size
        row_slot = places // group_size
        token_local = device_perm[inner % column_count] * TOK_DEV + inner // column_count
        slot_row = (row_slot + shifts[token_local]) % TOP
        chosen = EXP_COL * column_perm[block] + parity
        ids = jnp.zeros((group_size, TOP), jnp.int32).at[token_local, slot_row].set(chosen)
        slots = jnp.zeros((group_size, TOP), jnp.int32).at[token_local, slot_row].set(parity * SLOTS + rank)
        return (ids, slots)
    ids, slots = jax.vmap(one_group)(jax.random.split(key, group_count))
    return (ids.reshape(TOKENS, TOP), slots.reshape(TOKENS, TOP))


def draw_expert_ids(key, part):
    return routing_tables(key)[0]


def draw_slot_ids(key, part):
    return routing_tables(key)[1]


def touch_ends(drawn, rng, least, largest):
    longest = drawn.shape.index(max(drawn.shape))
    spots = []
    for shift in (0, 1):
        where = [jax.random.randint(jax.random.fold_in(rng, axis), (), 0, length) for axis, length in enumerate(drawn.shape)]
        where[longest] = (where[longest] + shift) % drawn.shape[longest]
        spots.append(tuple(where))
    return drawn.at[spots[0]].set(least).at[spots[1]].set(largest)


def block_levels(own_key, extent, cuts, low, top_value):
    gain = 1.0
    for dim, blocks in cuts:
        steps = jax.random.uniform(jax.random.fold_in(jax.random.fold_in(own_key, 6), dim), (blocks,), jnp.float32, low / len(cuts), top_value / len(cuts))
        gain = gain * jnp.repeat(jnp.exp(steps), extent[dim] // blocks).reshape((-1,) + (1,) * (len(extent) - 1 - dim))
    return gain


def bell_draw(stream_key, shape, width, limit, pieces=(), kind=jnp.bfloat16):
    array = jax.random.normal(stream_key, shape, jnp.float32) * width
    if len(pieces) > 0:
        array = block_levels(stream_key, shape, pieces, -0.22, 0.18) * array
    return jnp.clip(array, min=-limit, max=limit).astype(kind)


def setup_inputs(seed: int = 0) -> dict:
    splits = jax.random.split(jax.random.key(seed), 9)
    return {
        "tokens": bell_draw(splits[0], (TOKENS, D), 1.0, 6.0, ((0, 1024),)),
        "expert_ids": draw_expert_ids(jax.random.fold_in(splits[8], 71), 0),
        "gate_units": touch_ends(jax.random.randint(splits[2], (TOKENS, TOP), 1, 17), jax.random.fold_in(splits[2], 1), 1, 16).astype(jnp.int32),
        "slot_ids": draw_slot_ids(jax.random.fold_in(splits[8], 71), 0),
        "grad_out": bell_draw(splits[4], (TOKENS, D), 1.0, 6.0, ((0, 1024),)),
        "gate_weight": bell_draw(splits[5], (N_EXPERT, D, EXP_COL * F), D ** -0.5, 0.09375, ((0, 64), (2, 16))),
        "up_weight": bell_draw(splits[6], (N_EXPERT, D, EXP_COL * F), D ** -0.5, 0.09375, ((0, 64), (2, 16))),
        "down_weight": bell_draw(splits[7], (N_EXPERT, EXP_COL * F, D), F ** -0.5, 0.21875, ((0, 64), (1, 16))),
    }


def reference(tokens, expert_ids, gate_units, slot_ids, grad_out, gate_weight, up_weight, down_weight):
    model_width = tokens.shape[1]
    group_size = TOK_DEV * N_EXPERT
    hold_count = N_NODE // EXP_COL
    block_width = F // hold_count
    shares = gate_units.astype(jnp.float32)
    shares = shares / jnp.sum(shares, axis=1, keepdims=True)
    token_index = jnp.broadcast_to(jnp.arange(TOKENS, dtype=jnp.int32)[:, None], expert_ids.shape)
    group_index = token_index // group_size
    rank_index = slot_ids - (expert_ids % EXP_COL) * SLOTS
    table = jnp.zeros((EXPERTS, N_NODE, SLOTS), jnp.int32).at[expert_ids, group_index, rank_index].set(token_index + 1)
    share_table = jnp.zeros((EXPERTS, N_NODE, SLOTS), jnp.float32).at[expert_ids, group_index, rank_index].set(shares)
    gate_all = gate_weight.reshape(N_EXPERT, model_width, EXP_COL, F).transpose(0, 2, 1, 3).reshape(EXPERTS, model_width, F)
    up_all = up_weight.reshape(N_EXPERT, model_width, EXP_COL, F).transpose(0, 2, 1, 3).reshape(EXPERTS, model_width, F)
    down_all = down_weight.reshape(EXPERTS, F, model_width)
    highest = lax.Precision.HIGHEST

    def one_expert(carry, inputs):
        out_acc, back_acc = carry
        rows, row_share, w_gate, w_up, w_down = inputs
        rows = rows.reshape(-1)
        row_share = row_share.reshape(-1)
        valid = rows > 0
        picked = jnp.maximum(rows - 1, 0)
        row_x = jnp.where(valid[:, None], tokens[picked], jnp.zeros((), jnp.bfloat16))
        row_dy = (row_share[:, None] * grad_out[picked].astype(jnp.float32)).astype(jnp.bfloat16)
        gate_pre = jnp.dot(row_x, w_gate, preferred_element_type=jnp.float32)
        up_pre = jnp.dot(row_x, w_up, preferred_element_type=jnp.float32)
        sigma_gate = jax.nn.sigmoid(gate_pre)
        activ = gate_pre * sigma_gate
        hidden = (activ * up_pre).astype(jnp.bfloat16)
        row_count = hidden.shape[0]
        parts = jnp.einsum('rhf,hfd->hrd', hidden.astype(jnp.float32).reshape(row_count, hold_count, block_width),
                           w_down.astype(jnp.float32).reshape(hold_count, block_width, model_width), precision=highest)
        parts = lax.optimization_barrier(parts.astype(jnp.bfloat16))
        expert_out = jnp.sum(parts.astype(jnp.float32), axis=0).astype(jnp.bfloat16)
        grad_hidden = jnp.dot(row_dy, w_down.T, preferred_element_type=jnp.float32)
        grad_down = jnp.dot(hidden.T, row_dy, preferred_element_type=jnp.float32).astype(jnp.bfloat16)
        grad_gpre = (grad_hidden * up_pre * sigma_gate * (1.0 + gate_pre * (1.0 - sigma_gate))).astype(jnp.bfloat16)
        grad_upre = (grad_hidden * activ).astype(jnp.bfloat16)
        backs = jnp.einsum('rhf,dhf->hrd', grad_gpre.astype(jnp.float32).reshape(row_count, hold_count, block_width),
                           w_gate.astype(jnp.float32).reshape(model_width, hold_count, block_width), precision=highest)
        backs = backs + jnp.einsum('rhf,dhf->hrd', grad_upre.astype(jnp.float32).reshape(row_count, hold_count, block_width),
                                   w_up.astype(jnp.float32).reshape(model_width, hold_count, block_width), precision=highest)
        backs = lax.optimization_barrier(backs.astype(jnp.bfloat16))
        expert_back = jnp.sum(backs.astype(jnp.float32), axis=0).astype(jnp.bfloat16)
        out_acc = out_acc.at[picked].add(row_share[:, None] * expert_out.astype(jnp.float32))
        back_acc = back_acc.at[picked].add(jnp.where(valid[:, None], expert_back.astype(jnp.float32), jnp.float32(0.0)))
        return (out_acc, back_acc), grad_down

    start = (jnp.zeros((TOKENS, model_width), jnp.float32), jnp.zeros((TOKENS, model_width), jnp.float32))
    (out_acc, back_acc), grad_down = lax.scan(
        one_expert, start, (table, share_table, gate_all, up_all, down_all))
    grad_down = grad_down.reshape(N_EXPERT, EXP_COL * F, model_width)
    return out_acc.astype(jnp.bfloat16), back_acc.astype(jnp.bfloat16), grad_down
```

```python
import jax
import jax.numpy as jnp
from jax import lax
from jax.sharding import Mesh
from jax.sharding import PartitionSpec as P

EXP_COL = 2
BLOCK = ("yh", "zd")
CHIPS = ("yl", "x")
LANES = 128


def per_device(
    tokens, expert_ids, gate_units, slot_ids, grad_out, gate_weight, up_weight, down_weight
):
    bf16, f32 = jnp.bfloat16, jnp.float32
    tok_count, width = tokens.shape
    top_count = expert_ids.shape[1]
    za, zd, yh = lax.axis_size("za"), lax.axis_size("zd"), lax.axis_size("yh")
    yl, xs = lax.axis_size("yl"), lax.axis_size("x")
    capacity = 5 * tok_count * top_count // 8
    dests = yh * zd
    chips = yl * xs
    kinds = jnp.eye(2, dtype=f32)

    with jax.named_scope("spread"):
        meta = jnp.concatenate([expert_ids, slot_ids, gate_units], axis=1).astype(bf16)
        meta = jnp.pad(meta, ((0, tok_count), (0, LANES - 3 * top_count)))
        block = jnp.concatenate([tokens, grad_out], axis=0)
        spread = lax.all_gather(jnp.concatenate([block, meta], axis=1), "za", axis=0, tiled=True)

    with jax.named_scope("relay"):
        info = spread[:, width : width + 3 * top_count].reshape(za, 2, tok_count, -1)[:, 0]
        info = info.astype(jnp.int32)
        ids, slots, units = (
            info[..., :top_count],
            info[..., top_count : 2 * top_count],
            info[..., 2 * top_count :].astype(f32),
        )
        shares = units / jnp.sum(units, axis=-1, keepdims=True)
        lane = jnp.arange(dests, dtype=jnp.int32)
        column = (lane // zd) * (za * zd) + lax.axis_index("za") * zd + lane % zd
        match = (ids // EXP_COL)[None] == column[:, None, None, None]
        picks = jnp.sum(match.astype(f32), axis=-1)
        pick_share = jnp.sum(jnp.where(match, shares[None], f32(0.0)), axis=-1)
        row_share = jnp.sum(pick_share, axis=-1)
        row_slot = jnp.sum(jnp.where(match, slots[None] + 1, 0), axis=(-1, -2)) - 1
        sources = jnp.eye(za, dtype=f32)
        route = (
            picks[:, None, :, None, None, :]
            * sources[None, None, :, :, None, None]
            * kinds[None, :, None, None, :, None]
        ).reshape(dests * 2 * za, za * 2 * tok_count)
        scale = jnp.stack([jnp.ones_like(row_share), row_share], axis=1).reshape(-1, 1)
        rows = jnp.dot(route.astype(bf16), spread[:, :width], preferred_element_type=f32)
        rows = (rows * scale).astype(bf16)
        slot_rows = jnp.broadcast_to(row_slot[:, None, :, None], (dests, 2, za, LANES))
        slot_rows = slot_rows.reshape(-1, LANES).astype(bf16)
        sending = jnp.concatenate([rows, slot_rows], axis=1).reshape(dests, 2 * za, -1)
        got = lax.all_to_all(sending, BLOCK, split_axis=0, concat_axis=0, tiled=True)

    with jax.named_scope("dispatch"):
        got_slot = got[:, :za, width].astype(jnp.int32)
        position = jnp.arange(EXP_COL * capacity, dtype=jnp.int32).reshape(EXP_COL, capacity)
        placer = (got_slot[None, None] == position[:, :, None, None]).astype(f32)
        place = (
            placer[:, None, :, :, None, :] * kinds[None, :, None, None, :, None]
        ).reshape(EXP_COL, 2 * capacity, dests * 2 * za)
        packed = jnp.dot(
            place.reshape(EXP_COL * 2 * capacity, -1).astype(bf16),
            got[:, :, :width].reshape(dests * 2 * za, width),
            preferred_element_type=f32,
        ).astype(bf16)
        packed = packed.reshape(EXP_COL, 1, 2 * capacity, width)
        packed = jnp.broadcast_to(packed, (EXP_COL, xs, 2 * capacity, width))
        mine = lax.all_to_all(
            packed.reshape(chips, 2 * capacity, width), CHIPS, split_axis=0, concat_axis=0, tiled=True
        )
        swap = [(0, 1), (1, 0)]
        other = lax.ppermute(mine, "co", swap)

    with jax.named_scope("expert"):
        weights = jnp.concatenate([down_weight[0], gate_weight[0].T, up_weight[0].T], axis=0)
        hid = down_weight.shape[1]

        def half(rows_in):
            pre = lax.dot_general(
                rows_in, weights, (((1,), (1,)), ((), ())), preferred_element_type=f32
            ).reshape(chips, 2, capacity, 3 * hid)
            gate_pre = pre[:, 0, :, hid : 2 * hid]
            up_pre = pre[:, 0, :, 2 * hid :]
            grad_hidden = pre[:, 1, :, :hid]
            sigma = jax.nn.sigmoid(gate_pre)
            activ = gate_pre * sigma
            hidden = (activ * up_pre).astype(bf16)
            dgate = (grad_hidden * up_pre * sigma * (1.0 + gate_pre * (1.0 - sigma))).astype(bf16)
            dup = (grad_hidden * activ).astype(bf16)
            zero = jnp.zeros_like(hidden)
            mixer = jnp.stack(
                [
                    jnp.concatenate([hidden, zero, zero], axis=-1),
                    jnp.concatenate([zero, dgate, dup], axis=-1),
                ],
                axis=1,
            ).reshape(chips * 2 * capacity, 3 * hid)
            held = jnp.stack([zero, hidden], axis=1).reshape(chips * 2 * capacity, hid)
            return mixer, held

        flat_mine = mine.reshape(chips * 2 * capacity, width)
        flat_other = other.reshape(chips * 2 * capacity, width)
        mixer_mine, held_mine = half(flat_mine)
        mixer_other, held_other = half(flat_other)
        part_other = jnp.dot(mixer_other, weights, preferred_element_type=f32).astype(bf16)
        part_got = lax.ppermute(part_other, "co", swap)
        part_mine = jnp.dot(mixer_mine, weights, preferred_element_type=f32)
        grad_down = lax.dot_general(
            held_mine, flat_mine, (((0,), (0,)), ((), ())), preferred_element_type=f32
        ) + lax.dot_general(
            held_other, flat_other, (((0,), (0,)), ((), ())), preferred_element_type=f32
        )
        part = (part_mine + part_got.astype(f32)).astype(bf16)

    with jax.named_scope("combine"):
        parts = lax.all_to_all(
            part.reshape(chips, 2 * capacity, width), CHIPS, split_axis=0, concat_axis=0, tiled=True
        )
        gather = jnp.broadcast_to(
            place[:, None], (EXP_COL, xs, 2 * capacity, dests * 2 * za)
        ).reshape(chips * 2 * capacity, -1)
        back_rows = lax.dot_general(
            gather.astype(bf16),
            parts.reshape(chips * 2 * capacity, width),
            (((0,), (0,)), ((), ())),
            preferred_element_type=f32,
        ).astype(bf16)
        home = lax.all_to_all(
            back_rows.reshape(dests, 2 * za, width), BLOCK, split_axis=0, concat_axis=0, tiled=True
        ).reshape(dests * 2 * za, width)

    with jax.named_scope("sum"):
        weigh = jnp.stack([pick_share, picks], axis=1)
        weigh = (
            weigh.transpose(2, 1, 3, 0)[:, :, :, :, None, None]
            * sources[:, None, None, None, None, :]
            * kinds[None, :, None, None, :, None]
        ).reshape(za * 2 * tok_count, dests * 2 * za)
        high = lax.reduce_precision(weigh, 8, 7)
        rest = weigh - high
        middle = lax.reduce_precision(rest, 8, 7)
        low = rest - middle
        split = jnp.concatenate([high, middle, low], axis=0).astype(bf16)
        sums = jnp.dot(split, home, preferred_element_type=f32).reshape(3, -1, width)
        sums = (sums[0] + (sums[1] + sums[2])).astype(bf16)
        blocks = lax.all_to_all(
            sums.reshape(za, 2 * tok_count, width), "za", split_axis=0, concat_axis=0, tiled=True
        )
        total = jnp.sum(blocks.astype(f32), axis=0).astype(bf16)
    return total[:tok_count], total[tok_count:], grad_down.astype(bf16)[None]


def solution(mesh):
    columns = mesh.shape["expert"]
    zd = min(4, columns // 4)
    za = columns // (2 * zd)
    names = ("yl", "x", "co", "yh", "za", "zd")
    chips = mesh.shape["node"] // 4
    fine = Mesh(mesh.devices.reshape(2, chips, 2, 2, za, zd), names)
    node, expert = names[:3], names[3:]
    rows = P(names, None)
    return jax.shard_map(
        per_device,
        mesh=fine,
        in_specs=(rows,) * 5 + (P(expert, None, node),) * 2 + (P(expert, node, None),),
        out_specs=(rows, rows, P(expert, node, None)),
        check_vma=False,
    )
```

```python
import jax
import jax.numpy as jnp
from jax import lax
from jax.sharding import Mesh
from jax.sharding import PartitionSpec as P

EXP_COL = 2
NAMES = ("yl", "x", "co", "yh", "za", "zd")
CHIPS = ("yl", "x")
LANES = 128


def block_groups(yl, xs, yh, za, zd):
    depth, shift = za * zd, zd // 2
    groups = []
    for chip in range(yl * xs):
        for core in range(2):
            for first in range(0, depth, zd):
                zs = [(first + core * shift + step) % depth for step in range(zd)]
                groups.append([((chip * 2 + core) * yh + hi) * depth + z for hi in range(yh) for z in zs])
    return groups


def per_device(
    tokens, expert_ids, gate_units, slot_ids, grad_out, gate_weight, up_weight, down_weight
):
    bf16, f32 = jnp.bfloat16, jnp.float32
    tok_count, width = tokens.shape
    top_count = expert_ids.shape[1]
    za, zd, yh = lax.axis_size("za"), lax.axis_size("zd"), lax.axis_size("yh")
    yl, xs = lax.axis_size("yl"), lax.axis_size("x")
    capacity = 5 * tok_count * top_count // 8
    dests = yh * zd
    chips = yl * xs
    kinds = jnp.eye(2, dtype=f32)
    groups = block_groups(yl, xs, yh, za, zd)

    def exchange(rows_out):
        return lax.all_to_all(
            rows_out, NAMES, split_axis=0, concat_axis=0, axis_index_groups=groups, tiled=True
        )

    with jax.named_scope("spread"):
        meta = jnp.concatenate([expert_ids, slot_ids, gate_units], axis=1)
        meta = lax.optimization_barrier(meta).astype(bf16)
        meta = jnp.pad(meta, ((0, tok_count), (0, LANES - 3 * top_count)))
        block = jnp.concatenate([tokens, grad_out], axis=0)
        spread = lax.all_gather(jnp.concatenate([block, meta], axis=1), "za", axis=0, tiled=True)

    with jax.named_scope("relay"):
        info = spread[:, width : width + 3 * top_count].reshape(za, 2, tok_count, -1)[:, 0]
        info = info.astype(jnp.int32)
        ids, slots, units = (
            info[..., :top_count],
            info[..., top_count : 2 * top_count],
            info[..., 2 * top_count :].astype(f32),
        )
        shares = units / jnp.sum(units, axis=-1, keepdims=True)
        lane = jnp.arange(dests, dtype=jnp.int32)
        depth, shift = za * zd, lax.axis_index("co") * (zd // 2)
        own = (lax.axis_index("za") * zd + lax.axis_index("zd") + depth - shift) % depth
        column = (lane // zd) * depth + (own // zd * zd + shift + lane % zd) % depth
        match = (ids // EXP_COL)[None] == column[:, None, None, None]
        picks = jnp.sum(match.astype(f32), axis=-1)
        pick_share = jnp.sum(jnp.where(match, shares[None], f32(0.0)), axis=-1)
        row_share = jnp.sum(pick_share, axis=-1)
        row_slot = jnp.sum(jnp.where(match, slots[None] + 1, 0), axis=(-1, -2)) - 1
        sources = jnp.eye(za, dtype=f32)
        route = (
            picks[:, None, :, None, None, :]
            * sources[None, None, :, :, None, None]
            * kinds[None, :, None, None, :, None]
        ).reshape(dests * 2 * za, za * 2 * tok_count)
        scale = jnp.stack([jnp.ones_like(row_share), row_share], axis=1).reshape(-1, 1)
        rows = jnp.dot(route.astype(bf16), spread[:, :width], preferred_element_type=f32)
        rows = (rows * scale).astype(bf16)
        slot_rows = jnp.broadcast_to(row_slot[:, None, :, None], (dests, 2, za, LANES))
        slot_rows = slot_rows.reshape(-1, LANES).astype(bf16)
        sending = jnp.concatenate([rows, slot_rows], axis=1).reshape(dests, 2 * za, -1)
        weights = jnp.concatenate([down_weight[0], gate_weight[0].T, up_weight[0].T], axis=0)
        got, weights = lax.optimization_barrier((exchange(sending), weights))

    with jax.named_scope("dispatch"):
        got_slot = got[:, :za, width].astype(jnp.int32)
        position = jnp.arange(EXP_COL * capacity, dtype=jnp.int32).reshape(EXP_COL, capacity)
        placer = (got_slot[None, None] == position[:, :, None, None]).astype(f32)
        place = (
            placer[:, None, :, :, None, :] * kinds[None, :, None, None, :, None]
        ).reshape(EXP_COL, 2 * capacity, dests * 2 * za)
        packed = jnp.dot(
            place.reshape(EXP_COL * 2 * capacity, -1).astype(bf16),
            got[:, :, :width].reshape(dests * 2 * za, width),
            preferred_element_type=f32,
        ).astype(bf16)
        packed = packed.reshape(EXP_COL, 1, 2 * capacity, width)
        packed = jnp.broadcast_to(packed, (EXP_COL, xs, 2 * capacity, width))
        mine = lax.all_to_all(
            packed.reshape(chips, 2 * capacity, width), CHIPS, split_axis=0, concat_axis=0, tiled=True
        )
        swap = [(0, 1), (1, 0)]
        other = lax.ppermute(mine, "co", swap)

    with jax.named_scope("expert"):
        hid = down_weight.shape[1]

        def half(rows_in):
            pre = lax.dot_general(
                rows_in, weights, (((1,), (1,)), ((), ())), preferred_element_type=f32
            )
            pre = lax.optimization_barrier(pre).reshape(chips, 2, capacity, 3 * hid)
            gate_pre = pre[:, 0, :, hid : 2 * hid]
            up_pre = pre[:, 0, :, 2 * hid :]
            grad_hidden = pre[:, 1, :, :hid]
            sigma = jax.nn.sigmoid(gate_pre)
            activ = gate_pre * sigma
            hidden = (activ * up_pre).astype(bf16)
            dgate = (grad_hidden * up_pre * sigma * (1.0 + gate_pre * (1.0 - sigma))).astype(bf16)
            dup = (grad_hidden * activ).astype(bf16)
            zero = jnp.zeros_like(hidden)
            mixer = jnp.stack(
                [
                    jnp.concatenate([hidden, zero, zero], axis=-1),
                    jnp.concatenate([zero, dgate, dup], axis=-1),
                ],
                axis=1,
            ).reshape(chips * 2 * capacity, 3 * hid)
            held = jnp.stack([zero, hidden], axis=1).reshape(chips * 2 * capacity, hid)
            return mixer, held

        flat_mine = mine.reshape(chips * 2 * capacity, width)
        flat_other = other.reshape(chips * 2 * capacity, width)
        mixer_mine, held_mine = half(flat_mine)
        mixer_other, held_other = half(flat_other)
        pieces, wide = [], width // 2
        for cut in (slice(0, wide), slice(wide, width)):
            part_other = jnp.dot(mixer_other, weights[:, cut], preferred_element_type=f32)
            part_got = lax.ppermute(part_other.astype(bf16), "co", swap)
            part_mine = jnp.dot(mixer_mine, weights[:, cut], preferred_element_type=f32)
            pieces.append((part_mine + part_got.astype(f32)).astype(bf16))
        grad_down = lax.dot_general(
            held_mine, flat_mine, (((0,), (0,)), ((), ())), preferred_element_type=f32
        ) + lax.dot_general(
            held_other, flat_other, (((0,), (0,)), ((), ())), preferred_element_type=f32
        )
        part = jnp.concatenate(pieces, axis=1)

    with jax.named_scope("combine"):
        parts = lax.all_to_all(
            part.reshape(chips, 2 * capacity, width), CHIPS, split_axis=0, concat_axis=0, tiled=True
        )
        gather = jnp.broadcast_to(
            place[:, None], (EXP_COL, xs, 2 * capacity, dests * 2 * za)
        ).reshape(chips * 2 * capacity, -1)
        gather = lax.optimization_barrier(gather.T.astype(bf16))
        back_rows = lax.dot_general(
            gather,
            parts.reshape(chips * 2 * capacity, width),
            (((1,), (0,)), ((), ())),
            preferred_element_type=f32,
        ).astype(bf16)
        home = exchange(back_rows.reshape(dests, 2 * za, width)).reshape(dests * 2 * za, width)

    with jax.named_scope("sum"):
        weigh = jnp.stack([pick_share, picks], axis=1)
        weigh = (
            weigh.transpose(2, 1, 3, 0)[:, :, :, :, None, None]
            * sources[:, None, None, None, None, :]
            * kinds[None, :, None, None, :, None]
        ).reshape(za * 2 * tok_count, dests * 2 * za)
        high = lax.reduce_precision(weigh, 8, 7)
        rest = weigh - high
        middle = lax.reduce_precision(rest, 8, 7)
        low = rest - middle
        split = jnp.concatenate([high, middle, low], axis=0).astype(bf16)
        sums = jnp.dot(split, home, preferred_element_type=f32).reshape(3, -1, width)
        sums = (sums[0] + (sums[1] + sums[2])).astype(bf16)
        blocks = lax.all_to_all(
            sums.reshape(za, 2 * tok_count, width), "za", split_axis=0, concat_axis=0, tiled=True
        )
        total = jnp.sum(blocks.astype(f32), axis=0).astype(bf16)
    return total[:tok_count], total[tok_count:], grad_down.astype(bf16)[None]


def solution(mesh):
    columns = mesh.shape["expert"]
    zd = min(4, columns // 4)
    za = columns // (2 * zd)
    names = NAMES
    chips = mesh.shape["node"] // 4
    fine = Mesh(mesh.devices.reshape(2, chips, 2, 2, za, zd), names)
    node, expert = names[:3], names[3:]
    rows = P(names, None)
    return jax.shard_map(
        per_device,
        mesh=fine,
        in_specs=(rows,) * 5 + (P(expert, None, node),) * 2 + (P(expert, node, None),),
        out_specs=(rows, rows, P(expert, node, None)),
        check_vma=False,
    )
```

```python
import functools

import jax
import jax.numpy as jnp
from jax import lax
from jax.experimental import pallas as pl
from jax.experimental.pallas import tpu as pltpu
from jax.sharding import Mesh
from jax.sharding import PartitionSpec as P

EXP_COL = 2
NAMES = ("yl", "x", "co", "yh", "za", "zd")
CHIPS = ("yl", "x")
LANES = 128


def block_groups(yl, xs, yh, za, zd):
    depth, shift = za * zd, zd // 2
    groups = []
    for chip in range(yl * xs):
        for core in range(2):
            for first in range(0, depth, zd):
                zs = [(first + core * shift + step) % depth for step in range(zd)]
                groups.append([((chip * 2 + core) * yh + hi) * depth + z for hi in range(yh) for z in zs])
    return groups


def expert_kernel(capacity, rows_ref, weights_ref, out_ref, held_ref):
    bf16, f32 = jnp.bfloat16, jnp.float32
    count, width = rows_ref.shape
    pre = lax.dot_general(
        rows_ref[...], weights_ref[...], (((1,), (1,)), ((), ())), preferred_element_type=f32
    )
    gate_pre, up_pre = pre[:, LANES : 2 * LANES], pre[:, 2 * LANES :]
    grad_hidden = pltpu.roll(pre[:, :LANES], count - capacity, 0)
    row = lax.broadcasted_iota(jnp.int32, (count, LANES), 0)
    first = lax.rem(row, 2 * capacity) < capacity
    sigma = 1.0 / (1.0 + jnp.exp(-gate_pre))
    activ = gate_pre * sigma
    hidden = jnp.where(first, activ * up_pre, 0.0)
    dgate = grad_hidden * up_pre * sigma * (1.0 + gate_pre * (1.0 - sigma))
    dgate = pltpu.roll(jnp.where(first, dgate, 0.0), capacity, 0)
    dup = pltpu.roll(jnp.where(first, grad_hidden * activ, 0.0), capacity, 0)
    held_ref[...] = pltpu.roll(hidden, capacity, 0).astype(bf16)
    mixer = jnp.concatenate([hidden.astype(bf16), dgate.astype(bf16), dup.astype(bf16)], axis=1)
    step = min(width, 512)
    for at in range(0, width, step):
        out_ref[:, at : at + step] = jnp.dot(
            mixer, weights_ref[:, at : at + step], preferred_element_type=f32
        ).astype(bf16)


def expert_half(rows, weights, capacity):
    count, width = rows.shape
    return pl.pallas_call(
        functools.partial(expert_kernel, capacity),
        out_shape=(
            jax.ShapeDtypeStruct((count, width), jnp.bfloat16),
            jax.ShapeDtypeStruct((count, LANES), jnp.bfloat16),
        ),
        in_specs=[pl.BlockSpec(memory_space=pltpu.VMEM)] * 2,
        out_specs=(pl.BlockSpec(memory_space=pltpu.VMEM),) * 2,
        compiler_params=pltpu.CompilerParams(vmem_limit_bytes=24 << 20),
        cost_estimate=pl.CostEstimate(
            flops=4 * count * width * 3 * LANES,
            bytes_accessed=4 * count * width + 6 * LANES * width,
            transcendentals=count * LANES,
        ),
    )(rows, weights)


def per_device(
    tokens, expert_ids, gate_units, slot_ids, grad_out, gate_weight, up_weight, down_weight
):
    bf16, f32 = jnp.bfloat16, jnp.float32
    tok_count, width = tokens.shape
    top_count = expert_ids.shape[1]
    za, zd, yh = lax.axis_size("za"), lax.axis_size("zd"), lax.axis_size("yh")
    yl, xs = lax.axis_size("yl"), lax.axis_size("x")
    capacity = 5 * tok_count * top_count // 8
    dests = yh * zd
    chips = yl * xs
    kinds = jnp.eye(2, dtype=f32)
    groups = block_groups(yl, xs, yh, za, zd)

    def exchange(rows_out):
        return lax.all_to_all(
            rows_out, NAMES, split_axis=0, concat_axis=0, axis_index_groups=groups, tiled=True
        )

    with jax.named_scope("spread"):
        meta = jnp.concatenate([expert_ids, slot_ids, gate_units], axis=1)
        meta = lax.optimization_barrier(meta).astype(bf16)
        meta = jnp.pad(meta, ((0, tok_count), (0, LANES - 3 * top_count)))
        block = jnp.concatenate([tokens, grad_out], axis=0)
        spread = lax.all_gather(jnp.concatenate([block, meta], axis=1), "za", axis=0, tiled=True)

    with jax.named_scope("relay"):
        info = spread[:, width : width + 3 * top_count].reshape(za, 2, tok_count, -1)[:, 0]
        info = info.astype(jnp.int32)
        ids, slots, units = (
            info[..., :top_count],
            info[..., top_count : 2 * top_count],
            info[..., 2 * top_count :].astype(f32),
        )
        shares = units / jnp.sum(units, axis=-1, keepdims=True)
        lane = jnp.arange(dests, dtype=jnp.int32)
        depth, shift = za * zd, lax.axis_index("co") * (zd // 2)
        own = (lax.axis_index("za") * zd + lax.axis_index("zd") + depth - shift) % depth
        column = (lane // zd) * depth + (own // zd * zd + shift + lane % zd) % depth
        match = (ids // EXP_COL)[None] == column[:, None, None, None]
        picks = jnp.sum(match.astype(f32), axis=-1)
        pick_share = jnp.sum(jnp.where(match, shares[None], f32(0.0)), axis=-1)
        row_share = jnp.sum(pick_share, axis=-1)
        row_slot = jnp.sum(jnp.where(match, slots[None] + 1, 0), axis=(-1, -2)) - 1
        sources = jnp.eye(za, dtype=f32)
        route = (
            picks[:, None, :, None, None, :]
            * sources[None, None, :, :, None, None]
            * kinds[None, :, None, None, :, None]
        ).reshape(dests * 2 * za, za * 2 * tok_count)
        scale = jnp.stack([jnp.ones_like(row_share), row_share], axis=1).reshape(-1, 1)
        rows = jnp.dot(route.astype(bf16), spread[:, :width], preferred_element_type=f32)
        rows = (rows * scale).astype(bf16)
        slot_rows = jnp.broadcast_to(row_slot[:, None, :, None], (dests, 2, za, LANES))
        slot_rows = slot_rows.reshape(-1, LANES).astype(bf16)
        sending = jnp.concatenate([rows, slot_rows], axis=1).reshape(dests, 2 * za, -1)
        got = exchange(sending)
        hid = down_weight.shape[1]
        pad = ((0, LANES - hid), (0, 0))
        weights = jnp.concatenate(
            [jnp.pad(w, pad) for w in (down_weight[0], gate_weight[0].T, up_weight[0].T)], axis=0
        )
        slot_part, weights = lax.optimization_barrier((got[:, :za, width:], weights))

    with jax.named_scope("dispatch"):
        got_slot = slot_part[:, :, 0].astype(jnp.int32)
        position = jnp.arange(EXP_COL * capacity, dtype=jnp.int32).reshape(EXP_COL, capacity)
        placer = (got_slot[None, None] == position[:, :, None, None]).astype(f32)
        place = (
            placer[:, None, :, :, None, :] * kinds[None, :, None, None, :, None]
        ).reshape(EXP_COL, 2 * capacity, dests * 2 * za)
        packed = jnp.dot(
            place.reshape(EXP_COL * 2 * capacity, -1).astype(bf16),
            got[:, :, :width].reshape(dests * 2 * za, width),
            preferred_element_type=f32,
        ).astype(bf16)
        packed = packed.reshape(EXP_COL, 1, 2 * capacity, width)
        packed = jnp.broadcast_to(packed, (EXP_COL, xs, 2 * capacity, width))
        mine = lax.all_to_all(
            packed.reshape(chips, 2 * capacity, width), CHIPS, split_axis=0, concat_axis=0, tiled=True
        )
        swap = [(0, 1), (1, 0)]
        other = lax.ppermute(mine, "co", swap)

    with jax.named_scope("expert"):
        flat_mine = mine.reshape(chips * 2 * capacity, width)
        flat_other = other.reshape(chips * 2 * capacity, width)
        part_mine, held_mine = expert_half(flat_mine, weights, capacity)
        part_other, held_other = expert_half(flat_other, weights, capacity)
        part_got = lax.ppermute(part_other, "co", swap)
        part = (part_mine.astype(f32) + part_got.astype(f32)).astype(bf16)
        grad_down = lax.dot_general(
            held_mine, flat_mine, (((0,), (0,)), ((), ())), preferred_element_type=f32
        ) + lax.dot_general(
            held_other, flat_other, (((0,), (0,)), ((), ())), preferred_element_type=f32
        )
        grad_down = grad_down[:hid]

    with jax.named_scope("combine"):
        parts = lax.all_to_all(
            part.reshape(chips, 2 * capacity, width), CHIPS, split_axis=0, concat_axis=0, tiled=True
        )
        gather = jnp.broadcast_to(
            place[:, None], (EXP_COL, xs, 2 * capacity, dests * 2 * za)
        ).reshape(chips * 2 * capacity, -1)
        gather = lax.optimization_barrier(gather.T.astype(bf16))
        back_rows = lax.dot_general(
            gather,
            parts.reshape(chips * 2 * capacity, width),
            (((1,), (0,)), ((), ())),
            preferred_element_type=f32,
        ).astype(bf16)
        home = exchange(back_rows.reshape(dests, 2 * za, width)).reshape(dests * 2 * za, width)

    with jax.named_scope("sum"):
        weigh = jnp.stack([pick_share, picks], axis=1)
        weigh = (
            weigh.transpose(2, 1, 3, 0)[:, :, :, :, None, None]
            * sources[:, None, None, None, None, :]
            * kinds[None, :, None, None, :, None]
        ).reshape(za * 2 * tok_count, dests * 2 * za)
        high = lax.reduce_precision(weigh, 8, 7)
        rest = weigh - high
        middle = lax.reduce_precision(rest, 8, 7)
        low = rest - middle
        split = jnp.concatenate([high, middle, low], axis=0).astype(bf16)
        sums = jnp.dot(split, home, preferred_element_type=f32).reshape(3, -1, width)
        sums = (sums[0] + (sums[1] + sums[2])).astype(bf16)
        blocks = lax.all_to_all(
            sums.reshape(za, 2 * tok_count, width), "za", split_axis=0, concat_axis=0, tiled=True
        )
        total = jnp.sum(blocks.astype(f32), axis=0).astype(bf16)
    return total[:tok_count], total[tok_count:], grad_down.astype(bf16)[None]


def solution(mesh):
    columns = mesh.shape["expert"]
    zd = min(4, columns // 4)
    za = columns // (2 * zd)
    names = NAMES
    chips = mesh.shape["node"] // 4
    fine = Mesh(mesh.devices.reshape(2, chips, 2, 2, za, zd), names)
    node, expert = names[:3], names[3:]
    rows = P(names, None)
    return jax.shard_map(
        per_device,
        mesh=fine,
        in_specs=(rows,) * 5 + (P(expert, None, node),) * 2 + (P(expert, node, None),),
        out_specs=(rows, rows, P(expert, node, None)),
        check_vma=False,
    )
```

```python
import functools

import jax
import jax.numpy as jnp
from jax import lax
from jax.experimental import pallas as pl
from jax.experimental.pallas import tpu as pltpu
from jax.sharding import Mesh
from jax.sharding import PartitionSpec as P

EXP_COL = 2
NAMES = ("yl", "x", "co", "yh", "za", "zd")
CHIPS = ("yl", "x")
LANES = 128


def block_groups(yl, xs, yh, za, zd):
    depth, shift = za * zd, zd // 2
    groups = []
    for chip in range(yl * xs):
        for core in range(2):
            for first in range(0, depth, zd):
                zs = [(first + core * shift + step) % depth for step in range(zd)]
                groups.append([((chip * 2 + core) * yh + hi) * depth + z for hi in range(yh) for z in zs])
    return groups


def spread_groups(yl, xs, yh, za, zd):
    groups = []
    for chip in range(yl * xs):
        for core in range(2):
            for hi in range(yh):
                for kind in range(zd):
                    group = []
                    for step in range(za):
                        b = (step + core * zd + kind) % za
                        z = b * zd + (kind if b < za // 2 else kind ^ 1)
                        group.append(((chip * 2 + core) * yh + hi) * za * zd + z)
                    groups.append(group)
    return groups


def expert_kernel(capacity, rows_ref, weights_ref, out_ref, held_ref):
    bf16, f32 = jnp.bfloat16, jnp.float32
    count, width = rows_ref.shape
    pre = lax.dot_general(
        rows_ref[...], weights_ref[...], (((1,), (1,)), ((), ())), preferred_element_type=f32
    )
    gate_pre, up_pre = pre[:, LANES : 2 * LANES], pre[:, 2 * LANES :]
    grad_hidden = pltpu.roll(pre[:, :LANES], count - capacity, 0)
    row = lax.broadcasted_iota(jnp.int32, (count, LANES), 0)
    first = lax.rem(row, 2 * capacity) < capacity
    sigma = 1.0 / (1.0 + jnp.exp(-gate_pre))
    activ = gate_pre * sigma
    hidden = jnp.where(first, activ * up_pre, 0.0)
    dgate = grad_hidden * up_pre * sigma * (1.0 + gate_pre * (1.0 - sigma))
    dgate = pltpu.roll(jnp.where(first, dgate, 0.0), capacity, 0)
    dup = pltpu.roll(jnp.where(first, grad_hidden * activ, 0.0), capacity, 0)
    held_ref[...] = pltpu.roll(hidden, capacity, 0).astype(bf16)
    mixer = jnp.concatenate([hidden.astype(bf16), dgate.astype(bf16), dup.astype(bf16)], axis=1)
    step = min(width, 512)
    for at in range(0, width, step):
        out_ref[:, at : at + step] = jnp.dot(
            mixer, weights_ref[:, at : at + step], preferred_element_type=f32
        ).astype(bf16)


def expert_half(rows, weights, capacity):
    count, width = rows.shape
    return pl.pallas_call(
        functools.partial(expert_kernel, capacity),
        out_shape=(
            jax.ShapeDtypeStruct((count, width), jnp.bfloat16),
            jax.ShapeDtypeStruct((count, LANES), jnp.bfloat16),
        ),
        in_specs=[pl.BlockSpec(memory_space=pltpu.VMEM)] * 2,
        out_specs=(pl.BlockSpec(memory_space=pltpu.VMEM),) * 2,
        compiler_params=pltpu.CompilerParams(vmem_limit_bytes=24 << 20),
        cost_estimate=pl.CostEstimate(
            flops=4 * count * width * 3 * LANES,
            bytes_accessed=4 * count * width + 6 * LANES * width,
            transcendentals=count * LANES,
        ),
    )(rows, weights)


def per_device(
    tokens, expert_ids, gate_units, slot_ids, grad_out, gate_weight, up_weight, down_weight
):
    bf16, f32 = jnp.bfloat16, jnp.float32
    tok_count, width = tokens.shape
    top_count = expert_ids.shape[1]
    za, zd, yh = lax.axis_size("za"), lax.axis_size("zd"), lax.axis_size("yh")
    yl, xs = lax.axis_size("yl"), lax.axis_size("x")
    capacity = 5 * tok_count * top_count // 8
    dests = yh * zd
    chips = yl * xs
    kinds = jnp.eye(2, dtype=f32)
    groups = block_groups(yl, xs, yh, za, zd)
    far_groups = spread_groups(yl, xs, yh, za, zd)

    def exchange(rows_out):
        return lax.all_to_all(
            rows_out, NAMES, split_axis=0, concat_axis=0, axis_index_groups=groups, tiled=True
        )

    with jax.named_scope("spread"):
        meta = jnp.concatenate([expert_ids, slot_ids, gate_units], axis=1)
        meta = lax.optimization_barrier(meta).astype(bf16)
        meta = jnp.pad(meta, ((0, tok_count), (0, LANES - 3 * top_count)))
        block = jnp.concatenate([tokens, grad_out], axis=0)
        spread = lax.all_gather(
            jnp.concatenate([block, meta], axis=1),
            NAMES,
            axis=0,
            axis_index_groups=far_groups,
            tiled=True,
        )

    with jax.named_scope("relay"):
        info = spread[:, width : width + 3 * top_count].reshape(za, 2, tok_count, -1)[:, 0]
        info = info.astype(jnp.int32)
        ids, slots, units = (
            info[..., :top_count],
            info[..., top_count : 2 * top_count],
            info[..., 2 * top_count :].astype(f32),
        )
        shares = units / jnp.sum(units, axis=-1, keepdims=True)
        lane = jnp.arange(dests, dtype=jnp.int32)
        depth, shift = za * zd, lax.axis_index("co") * (zd // 2)
        own = (lax.axis_index("za") * zd + lax.axis_index("zd") + depth - shift) % depth
        column = (lane // zd) * depth + (own // zd * zd + shift + lane % zd) % depth
        match = (ids // EXP_COL)[None] == column[:, None, None, None]
        picks = jnp.sum(match.astype(f32), axis=-1)
        pick_share = jnp.sum(jnp.where(match, shares[None], f32(0.0)), axis=-1)
        row_share = jnp.sum(pick_share, axis=-1)
        row_slot = jnp.sum(jnp.where(match, slots[None] + 1, 0), axis=(-1, -2)) - 1
        sources = jnp.eye(za, dtype=f32)
        route = (
            picks[:, None, :, None, None, :]
            * sources[None, None, :, :, None, None]
            * kinds[None, :, None, None, :, None]
        ).reshape(dests * 2 * za, za * 2 * tok_count)
        scale = jnp.stack([jnp.ones_like(row_share), row_share], axis=1).reshape(-1, 1)
        rows = jnp.dot(route.astype(bf16), spread[:, :width], preferred_element_type=f32)
        rows = (rows * scale).astype(bf16)
        slot_rows = jnp.broadcast_to(row_slot[:, None, :, None], (dests, 2, za, LANES))
        slot_rows = slot_rows.reshape(-1, LANES).astype(bf16)
        sending = jnp.concatenate([rows, slot_rows], axis=1).reshape(dests, 2 * za, -1)
        got = exchange(sending)
        hid = down_weight.shape[1]
        pad = ((0, LANES - hid), (0, 0))
        weights = jnp.concatenate(
            [jnp.pad(w, pad) for w in (down_weight[0], gate_weight[0].T, up_weight[0].T)], axis=0
        )
        slot_part, weights = lax.optimization_barrier((got[:, :za, width:], weights))

    with jax.named_scope("dispatch"):
        got_slot = slot_part[:, :, 0].astype(jnp.int32)
        position = jnp.arange(EXP_COL * capacity, dtype=jnp.int32).reshape(EXP_COL, capacity)
        placer = (got_slot[None, None] == position[:, :, None, None]).astype(f32)
        place = (
            placer[:, None, :, :, None, :] * kinds[None, :, None, None, :, None]
        ).reshape(EXP_COL, 2 * capacity, dests * 2 * za)
        packed = jnp.dot(
            place.reshape(EXP_COL * 2 * capacity, -1).astype(bf16),
            got[:, :, :width].reshape(dests * 2 * za, width),
            preferred_element_type=f32,
        ).astype(bf16)
        packed = packed.reshape(EXP_COL, 1, 2 * capacity, width)
        packed = jnp.broadcast_to(packed, (EXP_COL, xs, 2 * capacity, width))
        mine = lax.all_to_all(
            packed.reshape(chips, 2 * capacity, width), CHIPS, split_axis=0, concat_axis=0, tiled=True
        )
        swap = [(0, 1), (1, 0)]
        other = lax.ppermute(mine, "co", swap)

    with jax.named_scope("expert"):
        flat_mine = mine.reshape(chips * 2 * capacity, width)
        flat_other = other.reshape(chips * 2 * capacity, width)
        part_mine, held_mine = expert_half(flat_mine, weights, capacity)
        part_other, held_other = expert_half(flat_other, weights, capacity)
        part_got = lax.ppermute(part_other, "co", swap)
        part = (part_mine.astype(f32) + part_got.astype(f32)).astype(bf16)
        grad_down = lax.dot_general(
            held_mine, flat_mine, (((0,), (0,)), ((), ())), preferred_element_type=f32
        ) + lax.dot_general(
            held_other, flat_other, (((0,), (0,)), ((), ())), preferred_element_type=f32
        )
        grad_down = grad_down[:hid]

    with jax.named_scope("combine"):
        parts = lax.all_to_all(
            part.reshape(chips, 2 * capacity, width), CHIPS, split_axis=0, concat_axis=0, tiled=True
        )
        gather = jnp.broadcast_to(
            place[:, None], (EXP_COL, xs, 2 * capacity, dests * 2 * za)
        ).reshape(chips * 2 * capacity, -1)
        gather = lax.optimization_barrier(gather.T.astype(bf16))
        back_rows = lax.dot_general(
            gather,
            parts.reshape(chips * 2 * capacity, width),
            (((1,), (0,)), ((), ())),
            preferred_element_type=f32,
        ).astype(bf16)
        home = exchange(back_rows.reshape(dests, 2 * za, width)).reshape(dests * 2 * za, width)

    with jax.named_scope("sum"):
        weigh = jnp.stack([pick_share, picks], axis=1)
        weigh = (
            weigh.transpose(2, 1, 3, 0)[:, :, :, :, None, None]
            * sources[:, None, None, None, None, :]
            * kinds[None, :, None, None, :, None]
        ).reshape(za * 2 * tok_count, dests * 2 * za)
        high = lax.reduce_precision(weigh, 8, 7)
        rest = weigh - high
        middle = lax.reduce_precision(rest, 8, 7)
        low = rest - middle
        split = jnp.concatenate([high, middle, low], axis=0).astype(bf16)
        sums = jnp.dot(split, home, preferred_element_type=f32).reshape(3, -1, width)
        sums = (sums[0] + (sums[1] + sums[2])).astype(bf16)
        blocks = lax.all_to_all(
            sums.reshape(za, 2 * tok_count, width),
            NAMES,
            split_axis=0,
            concat_axis=0,
            axis_index_groups=far_groups,
            tiled=True,
        )
        total = jnp.sum(blocks.astype(f32), axis=0).astype(bf16)
    return total[:tok_count], total[tok_count:], grad_down.astype(bf16)[None]


def solution(mesh):
    columns = mesh.shape["expert"]
    zd = min(4, columns // 4)
    za = columns // (2 * zd)
    names = NAMES
    chips = mesh.shape["node"] // 4
    fine = Mesh(mesh.devices.reshape(2, chips, 2, 2, za, zd), names)
    node, expert = names[:3], names[3:]
    rows = P(names, None)
    return jax.shard_map(
        per_device,
        mesh=fine,
        in_specs=(rows,) * 5 + (P(expert, None, node),) * 2 + (P(expert, node, None),),
        out_specs=(rows, rows, P(expert, node, None)),
        check_vma=False,
    )
```

```python
import functools

import jax
import jax.numpy as jnp
from jax import lax
from jax.experimental import pallas as pl
from jax.experimental.pallas import tpu as pltpu
from jax.sharding import Mesh
from jax.sharding import PartitionSpec as P

EXP_COL = 2
NAMES = ("yl", "x", "co", "yh", "za", "zd")
CHIPS = ("yl", "x")
LANES = 128


def block_groups(yl, xs, yh, za, zd):
    depth, shift = za * zd, zd // 2
    groups = []
    for chip in range(yl * xs):
        for core in range(2):
            for first in range(0, depth, zd):
                zs = [(first + core * shift + step) % depth for step in range(zd)]
                groups.append([((chip * 2 + core) * yh + hi) * depth + z for hi in range(yh) for z in zs])
    return groups


def spread_groups(yl, xs, yh, za, zd):
    groups = []
    for chip in range(yl * xs):
        for core in range(2):
            for hi in range(yh):
                for kind in range(zd):
                    group = []
                    for step in range(za):
                        b = (step + core * zd + kind) % za
                        z = b * zd + (kind if b < za // 2 else kind ^ 1)
                        group.append(((chip * 2 + core) * yh + hi) * za * zd + z)
                    groups.append(group)
    return groups


def expert_kernel(capacity, rows_ref, mine_ref, other_ref, out_ref, held_mine_ref, held_other_ref):
    bf16, f32 = jnp.bfloat16, jnp.float32
    count, width = rows_ref.shape
    row = lax.broadcasted_iota(jnp.int32, (count, LANES), 0)
    first = lax.rem(row, 2 * capacity) < capacity
    mixers = []
    for weights_ref, held_ref in ((mine_ref, held_mine_ref), (other_ref, held_other_ref)):
        pre = lax.dot_general(
            rows_ref[...], weights_ref[...], (((1,), (1,)), ((), ())), preferred_element_type=f32
        )
        gate_pre, up_pre = pre[:, LANES : 2 * LANES], pre[:, 2 * LANES :]
        grad_hidden = pltpu.roll(pre[:, :LANES], count - capacity, 0)
        sigma = 1.0 / (1.0 + jnp.exp(-gate_pre))
        activ = gate_pre * sigma
        hidden = jnp.where(first, activ * up_pre, 0.0)
        dgate = grad_hidden * up_pre * sigma * (1.0 + gate_pre * (1.0 - sigma))
        dgate = pltpu.roll(jnp.where(first, dgate, 0.0), capacity, 0)
        dup = pltpu.roll(jnp.where(first, grad_hidden * activ, 0.0), capacity, 0)
        held_ref[...] = pltpu.roll(hidden, capacity, 0).astype(bf16)
        mixers.append(
            jnp.concatenate([hidden.astype(bf16), dgate.astype(bf16), dup.astype(bf16)], axis=1)
        )
    step = min(width, 512)
    for at in range(0, width, step):
        cut = slice(at, at + step)
        total = jnp.dot(mixers[0], mine_ref[:, cut], preferred_element_type=f32)
        total += jnp.dot(mixers[1], other_ref[:, cut], preferred_element_type=f32)
        out_ref[:, cut] = total.astype(bf16)


def expert_pair(rows, mine, other, capacity):
    count, width = rows.shape
    vmem = pl.BlockSpec(memory_space=pltpu.VMEM)
    return pl.pallas_call(
        functools.partial(expert_kernel, capacity),
        out_shape=(
            jax.ShapeDtypeStruct((count, width), jnp.bfloat16),
            jax.ShapeDtypeStruct((count, LANES), jnp.bfloat16),
            jax.ShapeDtypeStruct((count, LANES), jnp.bfloat16),
        ),
        in_specs=[vmem] * 3,
        out_specs=(vmem,) * 3,
        compiler_params=pltpu.CompilerParams(vmem_limit_bytes=32 << 20),
        cost_estimate=pl.CostEstimate(
            flops=8 * count * width * 3 * LANES,
            bytes_accessed=4 * count * width + 12 * LANES * width,
            transcendentals=2 * count * LANES,
        ),
    )(rows, mine, other)


def per_device(
    tokens, expert_ids, gate_units, slot_ids, grad_out, gate_weight, up_weight, down_weight
):
    bf16, f32 = jnp.bfloat16, jnp.float32
    tok_count, width = tokens.shape
    top_count = expert_ids.shape[1]
    za, zd, yh = lax.axis_size("za"), lax.axis_size("zd"), lax.axis_size("yh")
    yl, xs = lax.axis_size("yl"), lax.axis_size("x")
    capacity = 5 * tok_count * top_count // 8
    dests = yh * zd
    chips = yl * xs
    kinds = jnp.eye(2, dtype=f32)
    groups = block_groups(yl, xs, yh, za, zd)
    far_groups = spread_groups(yl, xs, yh, za, zd)

    def exchange(rows_out):
        return lax.all_to_all(
            rows_out, NAMES, split_axis=0, concat_axis=0, axis_index_groups=groups, tiled=True
        )

    with jax.named_scope("spread"):
        meta = jnp.concatenate([expert_ids, slot_ids, gate_units], axis=1)
        meta = lax.optimization_barrier(meta).astype(bf16)
        meta = jnp.pad(meta, ((0, tok_count), (0, LANES - 3 * top_count)))
        block = jnp.concatenate([tokens, grad_out], axis=0)
        spread = lax.all_gather(
            jnp.concatenate([block, meta], axis=1),
            NAMES,
            axis=0,
            axis_index_groups=far_groups,
            tiled=True,
        )

    with jax.named_scope("relay"):
        info = spread[:, width : width + 3 * top_count].reshape(za, 2, tok_count, -1)[:, 0]
        info = info.astype(jnp.int32)
        ids, slots, units = (
            info[..., :top_count],
            info[..., top_count : 2 * top_count],
            info[..., 2 * top_count :].astype(f32),
        )
        shares = units / jnp.sum(units, axis=-1, keepdims=True)
        lane = jnp.arange(dests, dtype=jnp.int32)
        depth, shift = za * zd, lax.axis_index("co") * (zd // 2)
        own = (lax.axis_index("za") * zd + lax.axis_index("zd") + depth - shift) % depth
        column = (lane // zd) * depth + (own // zd * zd + shift + lane % zd) % depth
        match = (ids // EXP_COL)[None] == column[:, None, None, None]
        picks = jnp.sum(match.astype(f32), axis=-1)
        pick_share = jnp.sum(jnp.where(match, shares[None], f32(0.0)), axis=-1)
        row_share = jnp.sum(pick_share, axis=-1)
        row_slot = jnp.sum(jnp.where(match, slots[None] + 1, 0), axis=(-1, -2)) - 1
        sources = jnp.eye(za, dtype=f32)
        route = (
            picks[:, None, :, None, None, :]
            * sources[None, None, :, :, None, None]
            * kinds[None, :, None, None, :, None]
        ).reshape(dests * 2 * za, za * 2 * tok_count)
        scale = jnp.stack([jnp.ones_like(row_share), row_share], axis=1).reshape(-1, 1)
        rows = jnp.dot(route.astype(bf16), spread[:, :width], preferred_element_type=f32)
        rows = (rows * scale).astype(bf16)
        slot_rows = jnp.broadcast_to(row_slot[:, None, :, None], (dests, 2, za, LANES))
        slot_rows = slot_rows.reshape(-1, LANES).astype(bf16)
        sending = jnp.concatenate([rows, slot_rows], axis=1).reshape(dests, 2 * za, -1)
        got = exchange(sending)
        hid = down_weight.shape[1]
        pad = ((0, LANES - hid), (0, 0))
        weights = jnp.concatenate(
            [jnp.pad(w, pad) for w in (down_weight[0], gate_weight[0].T, up_weight[0].T)], axis=0
        )
        swap = [(0, 1), (1, 0)]
        weights_other = lax.ppermute(weights, "co", swap)
        slot_part, weights, weights_other = lax.optimization_barrier(
            (got[:, :za, width:], weights, weights_other)
        )

    with jax.named_scope("dispatch"):
        got_slot = slot_part[:, :, 0].astype(jnp.int32)
        position = jnp.arange(EXP_COL * capacity, dtype=jnp.int32).reshape(EXP_COL, capacity)
        placer = (got_slot[None, None] == position[:, :, None, None]).astype(f32)
        place = (
            placer[:, None, :, :, None, :] * kinds[None, :, None, None, :, None]
        ).reshape(EXP_COL, 2 * capacity, dests * 2 * za)
        packed = jnp.dot(
            place.reshape(EXP_COL * 2 * capacity, -1).astype(bf16),
            got[:, :, :width].reshape(dests * 2 * za, width),
            preferred_element_type=f32,
        ).astype(bf16)
        packed = packed.reshape(EXP_COL, 1, 2 * capacity, width)
        packed = jnp.broadcast_to(packed, (EXP_COL, xs, 2 * capacity, width))
        mine = lax.all_to_all(
            packed.reshape(chips, 2 * capacity, width), CHIPS, split_axis=0, concat_axis=0, tiled=True
        )

    with jax.named_scope("expert"):
        flat = mine.reshape(chips * 2 * capacity, width)
        part, held_mine, held_other = expert_pair(flat, weights, weights_other, capacity)

        def down_sum(held):
            return lax.dot_general(
                held, flat, (((0,), (0,)), ((), ())), preferred_element_type=f32
            )[:hid]

        grad_down = down_sum(held_mine) + lax.ppermute(down_sum(held_other), "co", swap)

    with jax.named_scope("combine"):
        parts = lax.all_to_all(
            part.reshape(chips, 2 * capacity, width), CHIPS, split_axis=0, concat_axis=0, tiled=True
        )
        gather = jnp.broadcast_to(
            place[:, None], (EXP_COL, xs, 2 * capacity, dests * 2 * za)
        ).reshape(chips * 2 * capacity, -1)
        gather = lax.optimization_barrier(gather.T.astype(bf16))
        back_rows = lax.dot_general(
            gather,
            parts.reshape(chips * 2 * capacity, width),
            (((1,), (0,)), ((), ())),
            preferred_element_type=f32,
        ).astype(bf16)
        home = exchange(back_rows.reshape(dests, 2 * za, width)).reshape(dests * 2 * za, width)

    with jax.named_scope("sum"):
        weigh = jnp.stack([pick_share, picks], axis=1)
        weigh = (
            weigh.transpose(2, 1, 3, 0)[:, :, :, :, None, None]
            * sources[:, None, None, None, None, :]
            * kinds[None, :, None, None, :, None]
        ).reshape(za * 2 * tok_count, dests * 2 * za)
        high = lax.reduce_precision(weigh, 8, 7)
        rest = weigh - high
        middle = lax.reduce_precision(rest, 8, 7)
        low = rest - middle
        split = jnp.concatenate([high, middle, low], axis=0).astype(bf16)
        sums = jnp.dot(split, home, preferred_element_type=f32).reshape(3, -1, width)
        sums = (sums[0] + (sums[1] + sums[2])).astype(bf16)
        blocks = lax.all_to_all(
            sums.reshape(za, 2 * tok_count, width),
            NAMES,
            split_axis=0,
            concat_axis=0,
            axis_index_groups=far_groups,
            tiled=True,
        )
        total = jnp.sum(blocks.astype(f32), axis=0).astype(bf16)
    return total[:tok_count], total[tok_count:], grad_down.astype(bf16)[None]


def solution(mesh):
    columns = mesh.shape["expert"]
    zd = min(4, columns // 4)
    za = columns // (2 * zd)
    names = NAMES
    chips = mesh.shape["node"] // 4
    fine = Mesh(mesh.devices.reshape(2, chips, 2, 2, za, zd), names)
    node, expert = names[:3], names[3:]
    rows = P(names, None)
    return jax.shard_map(
        per_device,
        mesh=fine,
        in_specs=(rows,) * 5 + (P(expert, None, node),) * 2 + (P(expert, node, None),),
        out_specs=(rows, rows, P(expert, node, None)),
        check_vma=False,
    )
```

```python
import functools

import jax
import jax.numpy as jnp
from jax import lax
from jax.experimental import pallas as pl
from jax.experimental.pallas import tpu as pltpu
from jax.sharding import Mesh
from jax.sharding import PartitionSpec as P

EXP_COL = 2
NAMES = ("yl", "x", "co", "yh", "za", "zd")
LANES = 128


def block_groups(yl, xs, yh, za, zd):
    depth, shift = za * zd, zd // 2
    groups = []
    for chip in range(yl * xs):
        for core in range(2):
            for first in range(0, depth, zd):
                zs = [(first + core * shift + step) % depth for step in range(zd)]
                groups.append([((chip * 2 + core) * yh + hi) * depth + z for hi in range(yh) for z in zs])
    return groups


def spread_groups(yl, xs, yh, za, zd):
    groups = []
    for chip in range(yl * xs):
        for core in range(2):
            for hi in range(yh):
                for kind in range(zd):
                    group = []
                    for step in range(za):
                        b = (step + core * zd + kind) % za
                        z = b * zd + (kind if b < za // 2 else kind ^ 1)
                        group.append(((chip * 2 + core) * yh + hi) * za * zd + z)
                    groups.append(group)
    return groups


def expert_kernel(capacity, rows_ref, weights_ref, out_ref, held_ref, total_ref):
    bf16, f32 = jnp.bfloat16, jnp.float32
    width, hid = rows_ref.shape[1], held_ref.shape[0]
    step_id = pl.program_id(0)
    pre = lax.dot_general(
        weights_ref[...], rows_ref[...], (((1,), (1,)), ((), ())), preferred_element_type=f32
    )
    lane = lax.broadcasted_iota(jnp.int32, (hid, LANES), 1)
    first = lax.rem(lane, 2 * capacity) < capacity
    grad_hidden = pltpu.roll(pre[:hid], LANES - capacity, 1)
    gate_pre, up_pre = pre[hid : 2 * hid], pre[2 * hid :]
    sigma = 1.0 / (1.0 + jnp.exp(-gate_pre))
    activ = gate_pre * sigma
    hidden = jnp.where(first, activ * up_pre, 0.0)
    dgate = grad_hidden * up_pre * sigma * (1.0 + gate_pre * (1.0 - sigma))
    dgate = pltpu.roll(jnp.where(first, dgate, 0.0), capacity, 1)
    dup = pltpu.roll(jnp.where(first, grad_hidden * activ, 0.0), capacity, 1)
    held_ref[...] = pltpu.roll(hidden, capacity, 1).astype(bf16)
    mixer = jnp.concatenate([hidden.astype(bf16), dgate.astype(bf16), dup.astype(bf16)], axis=0)
    step = min(width, 512)

    def products():
        for at in range(0, width, step):
            cut = slice(at, at + step)
            yield cut, lax.dot_general(
                mixer, weights_ref[:, cut], (((0,), (0,)), ((), ())), preferred_element_type=f32
            )

    @pl.when(step_id == 0)
    def _():
        for cut, product in products():
            total_ref[:, cut] = product

    @pl.when(step_id > 0)
    def _():
        for cut, product in products():
            total_ref[:, cut] += product

    @pl.when(step_id == pl.num_programs(0) - 1)
    def _():
        out_ref[...] = total_ref[...].astype(bf16)


def whole_expert(rows, weights, blocks, capacity):
    width = rows.shape[1]
    depth = weights.shape[0] // blocks
    return pl.pallas_call(
        functools.partial(expert_kernel, capacity),
        grid=(blocks,),
        out_shape=(
            jax.ShapeDtypeStruct((LANES, width), jnp.bfloat16),
            jax.ShapeDtypeStruct((blocks * depth // 3, LANES), jnp.bfloat16),
        ),
        in_specs=[
            pl.BlockSpec((LANES, width), lambda b: (0, 0)),
            pl.BlockSpec((depth, width), lambda b: (b, 0)),
        ],
        out_specs=(
            pl.BlockSpec((LANES, width), lambda b: (0, 0)),
            pl.BlockSpec((depth // 3, LANES), lambda b: (b, 0)),
        ),
        scratch_shapes=[pltpu.VMEM((LANES, width), jnp.float32)],
        compiler_params=pltpu.CompilerParams(vmem_limit_bytes=56 << 20),
        cost_estimate=pl.CostEstimate(
            flops=4 * LANES * width * blocks * depth,
            bytes_accessed=2 * blocks * depth * width + 4 * LANES * width,
            transcendentals=blocks * depth * LANES // 3,
        ),
    )(rows, weights)


def per_device(
    tokens, expert_ids, gate_units, slot_ids, grad_out, gate_weight, up_weight, down_weight
):
    bf16, f32 = jnp.bfloat16, jnp.float32
    tok_count, width = tokens.shape
    top_count = expert_ids.shape[1]
    za, zd, yh = lax.axis_size("za"), lax.axis_size("zd"), lax.axis_size("yh")
    yl, xs = lax.axis_size("yl"), lax.axis_size("x")
    capacity = 5 * tok_count * top_count // 8
    dests = yh * zd
    kinds = jnp.eye(2, dtype=f32)
    groups = block_groups(yl, xs, yh, za, zd)
    far_groups = spread_groups(yl, xs, yh, za, zd)

    def exchange(rows_out):
        return lax.all_to_all(
            rows_out, NAMES, split_axis=0, concat_axis=0, axis_index_groups=groups, tiled=True
        )

    with jax.named_scope("weights"):
        weights = jnp.concatenate([down_weight[0], gate_weight[0].T, up_weight[0].T], axis=0)
        weights = lax.all_gather(weights, ("x", "co"), axis=0, tiled=True)

    with jax.named_scope("spread"):
        meta = jnp.concatenate([expert_ids, slot_ids, gate_units], axis=1)
        meta = lax.optimization_barrier(meta).astype(bf16)
        meta = jnp.pad(meta, ((0, tok_count), (0, LANES - 3 * top_count)))
        block = jnp.concatenate([tokens, grad_out], axis=0)
        spread = lax.all_gather(
            jnp.concatenate([block, meta], axis=1),
            NAMES,
            axis=0,
            axis_index_groups=far_groups,
            tiled=True,
        )

    with jax.named_scope("relay"):
        info = spread[:, width : width + 3 * top_count].reshape(za, 2, tok_count, -1)[:, 0]
        info = info.astype(jnp.int32)
        ids, slots, units = (
            info[..., :top_count],
            info[..., top_count : 2 * top_count],
            info[..., 2 * top_count :].astype(f32),
        )
        shares = units / jnp.sum(units, axis=-1, keepdims=True)
        lane = jnp.arange(dests, dtype=jnp.int32)
        depth, shift = za * zd, lax.axis_index("co") * (zd // 2)
        own = (lax.axis_index("za") * zd + lax.axis_index("zd") + depth - shift) % depth
        column = (lane // zd) * depth + (own // zd * zd + shift + lane % zd) % depth
        match = (ids // EXP_COL)[None] == column[:, None, None, None]
        picks = jnp.sum(match.astype(f32), axis=-1)
        pick_share = jnp.sum(jnp.where(match, shares[None], f32(0.0)), axis=-1)
        row_share = jnp.sum(pick_share, axis=-1)
        row_slot = jnp.sum(jnp.where(match, slots[None] + 1, 0), axis=(-1, -2)) - 1
        sources = jnp.eye(za, dtype=f32)
        route = (
            picks[:, None, :, None, None, :]
            * sources[None, None, :, :, None, None]
            * kinds[None, :, None, None, :, None]
        ).reshape(dests * 2 * za, za * 2 * tok_count)
        scale = jnp.stack([jnp.ones_like(row_share), row_share], axis=1).reshape(-1, 1)
        rows = jnp.dot(route.astype(bf16), spread[:, :width], preferred_element_type=f32)
        rows = (rows * scale).astype(bf16)
        slot_rows = jnp.broadcast_to(row_slot[:, None, :, None], (dests, 2, za, LANES))
        slot_rows = slot_rows.reshape(-1, LANES).astype(bf16)
        sending = jnp.concatenate([rows, slot_rows], axis=1).reshape(dests, 2 * za, -1)
        got = exchange(sending)

    with jax.named_scope("dispatch"):
        got_slot = got[:, :za, width].astype(jnp.int32)
        parity = (lax.axis_index("yl") + jnp.arange(EXP_COL, dtype=jnp.int32)) % EXP_COL
        position = parity[:, None] * capacity + jnp.arange(capacity, dtype=jnp.int32)
        placer = (got_slot[None, None] == position[:, :, None, None]).astype(f32)
        place = (
            placer[:, None, :, :, None, :] * kinds[None, :, None, None, :, None]
        ).reshape(EXP_COL, 2 * capacity, dests * 2 * za)
        packed = jnp.dot(
            place.reshape(EXP_COL * 2 * capacity, -1).astype(bf16),
            got[:, :, :width].reshape(dests * 2 * za, width),
            preferred_element_type=f32,
        ).astype(bf16)
        swap = [(0, 1), (1, 0)]
        half = 2 * capacity
        theirs = lax.ppermute(packed[half:], "yl", swap)

    with jax.named_scope("expert"):
        spare = jnp.zeros((LANES - 2 * half, width), bf16)
        rows_in = jnp.concatenate([packed[:half], theirs, spare], axis=0)
        part, held = whole_expert(rows_in, weights, 2 * xs, capacity)
        down_part = jnp.dot(held, rows_in, preferred_element_type=f32).astype(bf16)
        grad_down = lax.psum_scatter(down_part, ("x", "co"), scatter_dimension=0, tiled=True)

    with jax.named_scope("combine"):
        back = lax.ppermute(part[half : 2 * half], "yl", swap)
        parts = jnp.concatenate([part[:half], back], axis=0)
        gather = place.reshape(EXP_COL * half, dests * 2 * za)
        back_rows = jnp.dot(
            gather.T.astype(bf16), parts, preferred_element_type=f32
        ).astype(bf16)
        home = exchange(back_rows.reshape(dests, 2 * za, width)).reshape(dests * 2 * za, width)

    with jax.named_scope("sum"):
        weigh = jnp.stack([pick_share, picks], axis=1)
        weigh = (
            weigh.transpose(2, 1, 3, 0)[:, :, :, :, None, None]
            * sources[:, None, None, None, None, :]
            * kinds[None, :, None, None, :, None]
        ).reshape(za * 2 * tok_count, dests * 2 * za)
        high = lax.reduce_precision(weigh, 8, 7)
        rest = weigh - high
        middle = lax.reduce_precision(rest, 8, 7)
        low = rest - middle
        split = jnp.concatenate([high, middle, low], axis=0).astype(bf16)
        sums = jnp.dot(split, home, preferred_element_type=f32).reshape(3, -1, width)
        sums = (sums[0] + (sums[1] + sums[2])).astype(bf16)
        blocks = lax.all_to_all(
            sums.reshape(za, 2 * tok_count, width),
            NAMES,
            split_axis=0,
            concat_axis=0,
            axis_index_groups=far_groups,
            tiled=True,
        )
        total = jnp.sum(blocks.astype(f32), axis=0).astype(bf16)
    return total[:tok_count], total[tok_count:], grad_down.astype(bf16)[None]


def solution(mesh):
    columns = mesh.shape["expert"]
    zd = min(4, columns // 4)
    za = columns // (2 * zd)
    names = NAMES
    chips = mesh.shape["node"] // 4
    fine = Mesh(mesh.devices.reshape(2, chips, 2, 2, za, zd), names)
    node, expert = names[:3], names[3:]
    rows = P(names, None)
    return jax.shard_map(
        per_device,
        mesh=fine,
        in_specs=(rows,) * 5 + (P(expert, None, node),) * 2 + (P(expert, node, None),),
        out_specs=(rows, rows, P(expert, node, None)),
        check_vma=False,
    )
```

```python
import functools

import jax
import jax.numpy as jnp
from jax import lax
from jax.experimental import pallas as pl
from jax.experimental.pallas import tpu as pltpu
from jax.sharding import Mesh
from jax.sharding import PartitionSpec as P

EXP_COL = 2
NAMES = ("yl", "x", "co", "yh", "za", "zd")
LANES = 128


def block_groups(yl, xs, yh, za, zd):
    depth, shift = za * zd, zd // 2
    groups = []
    for chip in range(yl * xs):
        for core in range(2):
            for first in range(0, depth, zd):
                zs = [(first + core * shift + step) % depth for step in range(zd)]
                groups.append([((chip * 2 + core) * yh + hi) * depth + z for hi in range(yh) for z in zs])
    return groups


def spread_groups(yl, xs, yh, za, zd):
    groups = []
    for chip in range(yl * xs):
        for core in range(2):
            for hi in range(yh):
                for kind in range(zd):
                    group = []
                    for step in range(za):
                        b = (step + core * zd + kind) % za
                        z = b * zd + (kind if b < za // 2 else kind ^ 1)
                        group.append(((chip * 2 + core) * yh + hi) * za * zd + z)
                    groups.append(group)
    return groups


def expert_kernel(capacity, rows_ref, weights_ref, out_ref, held_ref, total_ref):
    bf16, f32 = jnp.bfloat16, jnp.float32
    width, hid = rows_ref.shape[1], held_ref.shape[0]
    step_id = pl.program_id(0)
    pre = lax.dot_general(
        weights_ref[...], rows_ref[...], (((1,), (1,)), ((), ())), preferred_element_type=f32
    )
    lane = lax.broadcasted_iota(jnp.int32, (hid, LANES), 1)
    first = lax.rem(lane, 2 * capacity) < capacity
    grad_hidden = pltpu.roll(pre[:hid], LANES - capacity, 1)
    gate_pre, up_pre = pre[hid : 2 * hid], pre[2 * hid :]
    sigma = 1.0 / (1.0 + jnp.exp(-gate_pre))
    activ = gate_pre * sigma
    hidden = jnp.where(first, activ * up_pre, 0.0)
    dgate = grad_hidden * up_pre * sigma * (1.0 + gate_pre * (1.0 - sigma))
    dgate = pltpu.roll(jnp.where(first, dgate, 0.0), capacity, 1)
    dup = pltpu.roll(jnp.where(first, grad_hidden * activ, 0.0), capacity, 1)
    held_ref[...] = pltpu.roll(hidden, capacity, 1).astype(bf16)
    mixer = jnp.concatenate([hidden.astype(bf16), dgate.astype(bf16), dup.astype(bf16)], axis=0)
    step = min(width, 512)

    def products():
        for at in range(0, width, step):
            cut = slice(at, at + step)
            yield cut, lax.dot_general(
                mixer, weights_ref[:, cut], (((0,), (0,)), ((), ())), preferred_element_type=f32
            )

    @pl.when(step_id == 0)
    def _():
        for cut, product in products():
            total_ref[:, cut] = product

    @pl.when(step_id > 0)
    def _():
        for cut, product in products():
            total_ref[:, cut] += product

    @pl.when(step_id == pl.num_programs(0) - 1)
    def _():
        out_ref[...] = total_ref[...].astype(bf16)


def whole_expert(rows, weights, blocks, capacity):
    width = rows.shape[1]
    depth = weights.shape[0] // blocks
    return pl.pallas_call(
        functools.partial(expert_kernel, capacity),
        grid=(blocks,),
        out_shape=(
            jax.ShapeDtypeStruct((LANES, width), jnp.bfloat16),
            jax.ShapeDtypeStruct((blocks * depth // 3, LANES), jnp.bfloat16),
        ),
        in_specs=[
            pl.BlockSpec((LANES, width), lambda b: (0, 0)),
            pl.BlockSpec((depth, width), lambda b: (b, 0)),
        ],
        out_specs=(
            pl.BlockSpec((LANES, width), lambda b: (0, 0)),
            pl.BlockSpec((depth // 3, LANES), lambda b: (b, 0)),
        ),
        scratch_shapes=[pltpu.VMEM((LANES, width), jnp.float32)],
        compiler_params=pltpu.CompilerParams(vmem_limit_bytes=56 << 20),
        cost_estimate=pl.CostEstimate(
            flops=4 * LANES * width * blocks * depth,
            bytes_accessed=2 * blocks * depth * width + 4 * LANES * width,
            transcendentals=blocks * depth * LANES // 3,
        ),
    )(rows, weights)


def per_device(
    tokens, expert_ids, gate_units, slot_ids, grad_out, gate_weight, up_weight, down_weight
):
    bf16, f32 = jnp.bfloat16, jnp.float32
    tok_count, width = tokens.shape
    top_count = expert_ids.shape[1]
    za, zd, yh = lax.axis_size("za"), lax.axis_size("zd"), lax.axis_size("yh")
    yl, xs = lax.axis_size("yl"), lax.axis_size("x")
    capacity = 5 * tok_count * top_count // 8
    dests = yh * zd
    kinds = jnp.eye(2, dtype=f32)
    groups = block_groups(yl, xs, yh, za, zd)
    far_groups = spread_groups(yl, xs, yh, za, zd)

    def exchange(rows_out):
        return lax.all_to_all(
            rows_out, NAMES, split_axis=0, concat_axis=0, axis_index_groups=groups, tiled=True
        )

    with jax.named_scope("weights"):
        weights = jnp.concatenate([down_weight[0], gate_weight[0].T, up_weight[0].T], axis=0)
        weights = lax.all_gather(weights, ("x", "co"), axis=0, tiled=True)

    with jax.named_scope("spread"):
        meta = jnp.concatenate([expert_ids, slot_ids, gate_units], axis=1)
        meta = lax.optimization_barrier(meta).astype(bf16)
        meta = jnp.pad(meta, ((0, tok_count), (0, LANES - 3 * top_count)))
        block = jnp.concatenate([tokens, grad_out], axis=0)
        spread = lax.all_gather(
            jnp.concatenate([block, meta], axis=1),
            NAMES,
            axis=0,
            axis_index_groups=far_groups,
            tiled=True,
        )

    with jax.named_scope("relay"):
        info = spread[:, width : width + 3 * top_count].reshape(za, 2, tok_count, -1)[:, 0]
        info = info.astype(jnp.int32)
        ids, slots, units = (
            info[..., :top_count],
            info[..., top_count : 2 * top_count],
            info[..., 2 * top_count :].astype(f32),
        )
        shares = units / jnp.sum(units, axis=-1, keepdims=True)
        lane = jnp.arange(dests, dtype=jnp.int32)
        depth, shift = za * zd, lax.axis_index("co") * (zd // 2)
        own = (lax.axis_index("za") * zd + lax.axis_index("zd") + depth - shift) % depth
        column = (lane // zd) * depth + (own // zd * zd + shift + lane % zd) % depth
        match = (ids // EXP_COL)[None] == column[:, None, None, None]
        picks = jnp.sum(match.astype(f32), axis=-1)
        pick_share = jnp.sum(jnp.where(match, shares[None], f32(0.0)), axis=-1)
        row_share = jnp.sum(pick_share, axis=-1)
        row_slot = jnp.sum(jnp.where(match, slots[None] + 1, 0), axis=(-1, -2)) - 1
        sources = jnp.eye(za, dtype=f32)
        route = (
            picks[:, None, :, None, None, :]
            * sources[None, None, :, :, None, None]
            * kinds[None, :, None, None, :, None]
        ).reshape(dests * 2 * za, za * 2 * tok_count)
        scale = jnp.stack([jnp.ones_like(row_share), row_share], axis=1).reshape(-1, 1)
        rows = jnp.dot(route.astype(bf16), spread[:, :width], preferred_element_type=f32)
        rows = (rows * scale).astype(bf16)
        slot_rows = jnp.broadcast_to(row_slot[:, None, :, None], (dests, 2, za, LANES))
        slot_rows = slot_rows.reshape(-1, LANES).astype(bf16)
        sending = jnp.concatenate([rows, slot_rows], axis=1).reshape(dests, 2 * za, -1)
        got = exchange(sending)

    with jax.named_scope("dispatch"):
        got_slot = got[:, :za, width].astype(jnp.int32)
        parity = (lax.axis_index("yl") + jnp.arange(EXP_COL, dtype=jnp.int32)) % EXP_COL
        position = parity[:, None] * capacity + jnp.arange(capacity, dtype=jnp.int32)
        placer = (got_slot[None, None] == position[:, :, None, None]).astype(f32)
        place = (
            placer[:, None, :, :, None, :] * kinds[None, :, None, None, :, None]
        ).reshape(EXP_COL, 2 * capacity, dests * 2 * za)
        packed = jnp.dot(
            place.reshape(EXP_COL * 2 * capacity, -1).astype(bf16),
            got[:, :, :width].reshape(dests * 2 * za, width),
            preferred_element_type=f32,
        ).astype(bf16)
        swap = [(0, 1), (1, 0)]
        half = 2 * capacity
        theirs = lax.ppermute(packed[half:], "yl", swap)

    with jax.named_scope("expert"):
        spare = jnp.zeros((LANES - 2 * half, width), bf16)
        rows_in = jnp.concatenate([packed[:half], theirs, spare], axis=0)
        part, held = whole_expert(rows_in, weights, 2 * xs, capacity)

    with jax.named_scope("combine"):
        back = lax.ppermute(part[half : 2 * half], "yl", swap)
        parts = jnp.concatenate([part[:half], back], axis=0)
        gather = place.reshape(EXP_COL * half, dests * 2 * za)
        back_rows = jnp.dot(
            gather.T.astype(bf16), parts, preferred_element_type=f32
        ).astype(bf16)
        back_rows, held = lax.optimization_barrier((back_rows, held))
        home = exchange(back_rows.reshape(dests, 2 * za, width)).reshape(dests * 2 * za, width)

        down_part = jnp.dot(held, rows_in, preferred_element_type=f32).astype(bf16)
        grad_down = lax.psum_scatter(down_part, ("x", "co"), scatter_dimension=0, tiled=True)

    with jax.named_scope("sum"):
        own_kind = jnp.where(
            lax.axis_index("za") < za // 2, lax.axis_index("zd"), lax.axis_index("zd") ^ 1
        )
        place_far = (lax.axis_index("za") + za - (lax.axis_index("co") * zd + own_kind) % za) % za
        steps = jnp.arange(za, dtype=jnp.int32)
        partner = ((place_far ^ steps)[:, None] == steps[None, :]).astype(f32)
        weigh = jnp.stack([pick_share, picks], axis=1)
        weigh = (
            weigh.transpose(1, 3, 0, 2)[None, :, :, :, None, :]
            * partner[:, None, None, None, None, :]
            * kinds[None, :, None, None, :, None]
        ).reshape(za * 2 * tok_count, dests * 2 * za)
        high = lax.reduce_precision(weigh, 8, 7)
        rest = weigh - high
        middle = lax.reduce_precision(rest, 8, 7)
        low = rest - middle
        split = jnp.concatenate([high, middle, low], axis=0).astype(bf16)
        sums = jnp.dot(split, home, preferred_element_type=f32).reshape(3, -1, width)
        sums = (sums[0] + (sums[1] + sums[2])).astype(bf16)
        sums = sums.reshape(za, 2 * tok_count, width)
        blocks = [sums[0]]
        for step in range(1, za):
            pairs = [(g[at], g[at ^ step]) for g in far_groups for at in range(za)]
            blocks.append(lax.ppermute(sums[step], NAMES, pairs))
        total = sum(b.astype(f32) for b in blocks).astype(bf16)
    return total[:tok_count], total[tok_count:], grad_down.astype(bf16)[None]


def solution(mesh):
    columns = mesh.shape["expert"]
    zd = min(4, columns // 4)
    za = columns // (2 * zd)
    names = NAMES
    chips = mesh.shape["node"] // 4
    fine = Mesh(mesh.devices.reshape(2, chips, 2, 2, za, zd), names)
    node, expert = names[:3], names[3:]
    rows = P(names, None)
    return jax.shard_map(
        per_device,
        mesh=fine,
        in_specs=(rows,) * 5 + (P(expert, None, node),) * 2 + (P(expert, node, None),),
        out_specs=(rows, rows, P(expert, node, None)),
        check_vma=False,
    )
```

```python
import functools

import jax
import jax.numpy as jnp
from jax import lax
from jax.experimental import pallas as pl
from jax.experimental.pallas import tpu as pltpu
from jax.sharding import Mesh
from jax.sharding import PartitionSpec as P

EXP_COL = 2
NAMES = ("yl", "x", "co", "yh", "za", "zd")
LANES = 128
PAIR = 2


def block_groups(yl, xs, yh, za, zd):
    depth, shift = za * zd, zd // 2
    groups = []
    for chip in range(yl * xs):
        for core in range(2):
            for first in range(0, depth, zd):
                zs = [(first + core * shift + step) % depth for step in range(zd)]
                groups.append([((chip * 2 + core) * yh + hi) * depth + z for hi in range(yh) for z in zs])
    return groups


def spread_groups(yl, xs, yh, za, zd):
    groups = []
    for chip in range(yl * xs):
        for core in range(2):
            for hi in range(yh):
                for kind in range(zd):
                    group = []
                    for step in range(za):
                        b = (step + core * zd + kind) % za
                        z = b * zd + (kind if b < za // 2 else kind ^ 1)
                        group.append(((chip * 2 + core) * yh + hi) * za * zd + z)
                    groups.append(group)
    return groups


def expert_kernel(capacity, rows_ref, weights_ref, out_ref, held_ref, total_ref):
    bf16, f32 = jnp.bfloat16, jnp.float32
    width, hid = rows_ref.shape[1], held_ref.shape[0] // PAIR
    step_id = pl.program_id(0)
    products_in = lax.dot_general(
        weights_ref[...], rows_ref[...], (((1,), (1,)), ((), ())), preferred_element_type=f32
    )
    lane = lax.broadcasted_iota(jnp.int32, (hid, LANES), 1)
    first = lax.rem(lane, 2 * capacity) < capacity
    mixer = []
    for block in range(PAIR):
        pre = products_in[block * 3 * hid : (block + 1) * 3 * hid]
        grad_hidden = pltpu.roll(pre[:hid], LANES - capacity, 1)
        gate_pre, up_pre = pre[hid : 2 * hid], pre[2 * hid :]
        sigma = 1.0 / (1.0 + jnp.exp(-gate_pre))
        activ = gate_pre * sigma
        hidden = jnp.where(first, activ * up_pre, 0.0)
        dgate = grad_hidden * up_pre * sigma * (1.0 + gate_pre * (1.0 - sigma))
        dgate = pltpu.roll(jnp.where(first, dgate, 0.0), capacity, 1)
        dup = pltpu.roll(jnp.where(first, grad_hidden * activ, 0.0), capacity, 1)
        held_ref[block * hid : (block + 1) * hid, :] = pltpu.roll(hidden, capacity, 1).astype(bf16)
        mixer += [hidden.astype(bf16), dgate.astype(bf16), dup.astype(bf16)]
    mixer = jnp.concatenate(mixer, axis=0)
    step = min(width, 512)

    def products():
        for at in range(0, width, step):
            cut = slice(at, at + step)
            yield cut, lax.dot_general(
                mixer, weights_ref[:, cut], (((0,), (0,)), ((), ())), preferred_element_type=f32
            )

    @pl.when(step_id == 0)
    def _():
        for cut, product in products():
            total_ref[:, cut] = product

    @pl.when(step_id > 0)
    def _():
        for cut, product in products():
            total_ref[:, cut] += product

    @pl.when(step_id == pl.num_programs(0) - 1)
    def _():
        out_ref[...] = total_ref[...].astype(bf16)


def whole_expert(rows, weights, blocks, capacity):
    width = rows.shape[1]
    depth = weights.shape[0] // blocks
    return pl.pallas_call(
        functools.partial(expert_kernel, capacity),
        grid=(blocks // PAIR,),
        out_shape=(
            jax.ShapeDtypeStruct((LANES, width), jnp.bfloat16),
            jax.ShapeDtypeStruct((blocks * depth // 3, LANES), jnp.bfloat16),
        ),
        in_specs=[
            pl.BlockSpec((LANES, width), lambda b: (0, 0)),
            pl.BlockSpec((PAIR * depth, width), lambda b: (b, 0)),
        ],
        out_specs=(
            pl.BlockSpec((LANES, width), lambda b: (0, 0)),
            pl.BlockSpec((PAIR * depth // 3, LANES), lambda b: (b, 0)),
        ),
        scratch_shapes=[pltpu.VMEM((LANES, width), jnp.float32)],
        compiler_params=pltpu.CompilerParams(vmem_limit_bytes=56 << 20),
        cost_estimate=pl.CostEstimate(
            flops=4 * LANES * width * blocks * depth,
            bytes_accessed=2 * blocks * depth * width + 4 * LANES * width,
            transcendentals=blocks * depth * LANES // 3,
        ),
    )(rows, weights)


def per_device(
    tokens, expert_ids, gate_units, slot_ids, grad_out, gate_weight, up_weight, down_weight
):
    bf16, f32 = jnp.bfloat16, jnp.float32
    tok_count, width = tokens.shape
    top_count = expert_ids.shape[1]
    za, zd, yh = lax.axis_size("za"), lax.axis_size("zd"), lax.axis_size("yh")
    yl, xs = lax.axis_size("yl"), lax.axis_size("x")
    capacity = 5 * tok_count * top_count // 8
    dests = yh * zd
    kinds = jnp.eye(2, dtype=f32)
    groups = block_groups(yl, xs, yh, za, zd)
    far_groups = spread_groups(yl, xs, yh, za, zd)

    def exchange(rows_out):
        return lax.all_to_all(
            rows_out, NAMES, split_axis=0, concat_axis=0, axis_index_groups=groups, tiled=True
        )

    with jax.named_scope("weights"):
        weights = jnp.concatenate([down_weight[0], gate_weight[0].T, up_weight[0].T], axis=0)
        weights = lax.all_gather(weights, ("x", "co"), axis=0, tiled=True)

    with jax.named_scope("spread"):
        meta = jnp.concatenate([expert_ids, slot_ids, gate_units], axis=1)
        meta = lax.optimization_barrier(meta).astype(bf16)
        meta = jnp.pad(meta, ((0, tok_count), (0, LANES - 3 * top_count)))
        block = jnp.concatenate([tokens, grad_out], axis=0)
        spread = lax.all_gather(
            jnp.concatenate([block, meta], axis=1),
            NAMES,
            axis=0,
            axis_index_groups=far_groups,
            tiled=True,
        )

    with jax.named_scope("relay"):
        info = spread[:, width : width + 3 * top_count].reshape(za, 2, tok_count, -1)[:, 0]
        info = info.astype(jnp.int32)
        ids, slots, units = (
            info[..., :top_count],
            info[..., top_count : 2 * top_count],
            info[..., 2 * top_count :].astype(f32),
        )
        shares = units / jnp.sum(units, axis=-1, keepdims=True)
        lane = jnp.arange(dests, dtype=jnp.int32)
        depth, shift = za * zd, lax.axis_index("co") * (zd // 2)
        own = (lax.axis_index("za") * zd + lax.axis_index("zd") + depth - shift) % depth
        column = (lane // zd) * depth + (own // zd * zd + shift + lane % zd) % depth
        match = (ids // EXP_COL)[None] == column[:, None, None, None]
        picks = jnp.sum(match.astype(f32), axis=-1)
        pick_share = jnp.sum(jnp.where(match, shares[None], f32(0.0)), axis=-1)
        row_share = jnp.sum(pick_share, axis=-1)
        row_slot = jnp.sum(jnp.where(match, slots[None] + 1, 0), axis=(-1, -2)) - 1
        sources = jnp.eye(za, dtype=f32)
        route = (
            picks[:, None, :, None, None, :]
            * sources[None, None, :, :, None, None]
            * kinds[None, :, None, None, :, None]
        ).reshape(dests * 2 * za, za * 2 * tok_count)
        scale = jnp.stack([jnp.ones_like(row_share), row_share], axis=1).reshape(-1, 1)
        rows = jnp.dot(route.astype(bf16), spread[:, :width], preferred_element_type=f32)
        rows = (rows * scale).astype(bf16)
        slot_rows = jnp.broadcast_to(row_slot[:, None, :, None], (dests, 2, za, LANES))
        slot_rows = slot_rows.reshape(-1, LANES).astype(bf16)
        sending = jnp.concatenate([rows, slot_rows], axis=1).reshape(dests, 2 * za, -1)
        got = exchange(sending)

    with jax.named_scope("dispatch"):
        got_slot = got[:, :za, width].astype(jnp.int32)
        parity = (lax.axis_index("yl") + jnp.arange(EXP_COL, dtype=jnp.int32)) % EXP_COL
        position = parity[:, None] * capacity + jnp.arange(capacity, dtype=jnp.int32)
        placer = (got_slot[None, None] == position[:, :, None, None]).astype(f32)
        place = (
            placer[:, None, :, :, None, :] * kinds[None, :, None, None, :, None]
        ).reshape(EXP_COL, 2 * capacity, dests * 2 * za)
        packed = jnp.dot(
            place.reshape(EXP_COL * 2 * capacity, -1).astype(bf16),
            got[:, :, :width].reshape(dests * 2 * za, width),
            preferred_element_type=f32,
        ).astype(bf16)
        swap = [(0, 1), (1, 0)]
        half = 2 * capacity
        theirs = lax.ppermute(packed[half:], "yl", swap)

    with jax.named_scope("expert"):
        spare = jnp.zeros((LANES - 2 * half, width), bf16)
        rows_in = jnp.concatenate([packed[:half], theirs, spare], axis=0)
        part, held = whole_expert(rows_in, weights, 2 * xs, capacity)
        down_part = jnp.dot(held, rows_in, preferred_element_type=f32).astype(bf16)
        grad_down = lax.psum_scatter(down_part, ("x", "co"), scatter_dimension=0, tiled=True)

    with jax.named_scope("combine"):
        back = lax.ppermute(part[half : 2 * half], "yl", swap)
        parts = jnp.concatenate([part[:half], back], axis=0)
        gather = place.reshape(EXP_COL * half, dests * 2 * za)
        back_rows = jnp.dot(
            gather.T.astype(bf16), parts, preferred_element_type=f32
        ).astype(bf16)
        home = exchange(back_rows.reshape(dests, 2 * za, width)).reshape(dests * 2 * za, width)

    with jax.named_scope("sum"):
        weigh = jnp.stack([pick_share, picks], axis=1)
        weigh = (
            weigh.transpose(2, 1, 3, 0)[:, :, :, :, None, None]
            * sources[:, None, None, None, None, :]
            * kinds[None, :, None, None, :, None]
        ).reshape(za * 2 * tok_count, dests * 2 * za)
        high = lax.reduce_precision(weigh, 8, 7)
        rest = weigh - high
        middle = lax.reduce_precision(rest, 8, 7)
        low = rest - middle
        split = jnp.concatenate([high, middle, low], axis=0).astype(bf16)
        sums = jnp.dot(split, home, preferred_element_type=f32).reshape(3, -1, width)
        sums = (sums[0] + (sums[1] + sums[2])).astype(bf16)
        blocks = lax.all_to_all(
            sums.reshape(za, 2 * tok_count, width),
            NAMES,
            split_axis=0,
            concat_axis=0,
            axis_index_groups=far_groups,
            tiled=True,
        )
        total = jnp.sum(blocks.astype(f32), axis=0).astype(bf16)
    return total[:tok_count], total[tok_count:], grad_down.astype(bf16)[None]


def solution(mesh):
    columns = mesh.shape["expert"]
    zd = min(4, columns // 4)
    za = columns // (2 * zd)
    names = NAMES
    chips = mesh.shape["node"] // 4
    fine = Mesh(mesh.devices.reshape(2, chips, 2, 2, za, zd), names)
    node, expert = names[:3], names[3:]
    rows = P(names, None)
    return jax.shard_map(
        per_device,
        mesh=fine,
        in_specs=(rows,) * 5 + (P(expert, None, node),) * 2 + (P(expert, node, None),),
        out_specs=(rows, rows, P(expert, node, None)),
        check_vma=False,
    )
```
